512 devices in a mesh: snd: 32 (over z, core), freq: 4 (over x), mesh: 4 (over y).
Axes of the slice: x: 4, y: 4, z: 16, core: 2. Of those that a mesh axis runs over, the one named last changes fastest.
Arguments:
- source: float32 [32, 6, 32, 3072], P('snd', None, 'mesh'), may hold values from -6 to 6
- adjoint: float32 [32, 4, 6, 32, 3072], P('snd', 'freq', None, 'mesh'), may hold values from -3 to 3
- omegas: float32 [4], P('freq'), may hold values from 0.5 to 8
- background: float32 [3], replicated, may hold values from 0.1 to 1
- conductivity: float32 [8192, 384], P(('snd', 'mesh')), may hold values from 0.05 to 5
- block_owner: int32 [32, 768, 1], P('snd', 'mesh'), may hold values from 0 to 127; in each aligned block of 192 rows (0 to 191, 192 to 383, ..., all dimensions but the last counted through in order) at most 4 rows name the same one
- block_local: int32 [32, 768], P('snd', 'mesh'), may hold values from 0 to 63
- block_count: int32 [32], P('snd'), may hold values from 384 to 768
Outputs:
- field: float32 [32, 4, 6, 32, 3072], P('snd', 'freq', None, 'mesh')
- gradient: float32 [8192, 384], P(('snd', 'mesh'))
The draws below stay inside these ranges and needn't reach their ends.
Inputs may be any that keep to these rules, and one draw needn't show every extreme that they name: `block_owner`: among the 192 blocks of one device (aligned blocks of rows of one footprint) no owner appears more than 4 times, and some owner appears exactly 4 times in some device's blocks.
All inputs are finite; a program needn't handle non-finite values.
Results may differ from the reference program's by a relative error of at most 0.0003.
Values sent between devices are 32-bit elements; how exact they have to be, the bound alone decides.
A program may use at most 64 MiB of HBM per device.

```python
import math
import jax
import jax.numpy as jnp
import numpy as np
from jax import lax

NY = 64
NZ = 48
ITERS = 4
GB_DEV = 64
NXF = 32
FB_DEV = 192
FBLK = 768
SOUNDS = 32
NFREQ = 4
GBLK = 8192
CAP = 4
N_SND = 32
N_MESH = 4


def with_ends(array, key, least, top_value):
    index_at = [jax.random.randint(jax.random.fold_in(key, axis), (), 0, length) for axis, length in enumerate(array.shape)]
    longest = array.shape.index(max(array.shape))
    next_to = index_at[:longest] + [(index_at[longest] + 1) % array.shape[longest]] + index_at[longest + 1:]
    return array.at[tuple(index_at)].set(least).at[tuple(next_to)].set(top_value)


def shard_levels(own_key, shape, split, low, largest):
    gain, own = 1.0, jax.random.fold_in(own_key, 6)
    for dim, shards_of in split:
        heights = jnp.exp(jax.random.uniform(jax.random.fold_in(own, dim), (shards_of,), jnp.float32, low / len(split), largest / len(split)))
        gain = gain * jnp.repeat(heights, shape[dim] // shards_of).reshape([-1 if axis == dim else 1 for axis in range(len(shape))])
    return gain


def deal_out(stream_key, own, number, rows, number_of, top, reach, lean):
    order = jax.random.permutation(stream_key, number_of)
    packed, common = portions_of(number_of, rows * top, reach, lean, True), portions_of(number_of, rows * top, reach, lean, False)
    places = jnp.arange(number_of)

    def named(sizes, offset_by):
        used = int((sizes > 0).sum())
        fixed = max(1, used // 4)
        shifted = fixed + (places - fixed + offset_by * (used - fixed)) % max(1, number_of - fixed)
        return jnp.zeros((number_of,), jnp.int32).at[order[jnp.where(places < fixed, places, shifted)]].set(jnp.asarray(sizes, jnp.int32))

    sizes = jnp.where(number % 4 == 0, named(packed, number // 4), named(common, number - number // 4 - 1))
    mixed = jax.random.permutation(jax.random.fold_in(own, 3), number_of)
    source_of, receiver = mixed[0:number_of // 2 * 2:2], mixed[1:number_of // 2 * 2:2]
    room = jnp.minimum(sizes[source_of] - 1, reach - sizes[receiver]) // 2
    room = jnp.where((source_of == order[0]) | (receiver == order[0]) | (sizes[receiver] == 0), 0, jnp.maximum(room, 0))
    shifted = jax.random.randint(jax.random.fold_in(own, 4), (number_of // 2,), 0, 1 << 20) % (room + 1)
    sizes = sizes.at[source_of].add(-shifted).at[receiver].add(shifted)
    items = jnp.searchsorted(jnp.cumsum(sizes), jnp.arange(rows * top), side="right").astype(jnp.int32)
    table = items.reshape(top, rows).T
    table = table[jax.random.permutation(jax.random.fold_in(own, 1), rows)]
    offset_by = jax.random.randint(jax.random.fold_in(own, 2), (rows, 1), 0, top)
    return jnp.take_along_axis(table, (jnp.arange(top)[None, :] + offset_by) % top, axis=1)


def portions_of(number_of, total, most, lean, full):
    loads = [(1 << 20) // math.isqrt(grade ** lean) + 1 for grade in range(1, number_of + 1)]
    largest = most if full else min(most, max(-(-total // number_of), total * loads[0] // sum(loads)))
    least = 1 if total - largest >= number_of - 1 else 0
    counts, surplus = [largest] + [least] * (number_of - 1), total - largest - least * (number_of - 1)
    while surplus > 0:
        candidates = [i for i in range(1, number_of) if counts[i] < largest] or [i for i in range(1, number_of) if counts[i] < most]
        mass, left = sum([loads[i] for i in candidates]), surplus
        for i in candidates:
            extra = min(most - counts[i], max(1, left * loads[i] // mass), surplus)
            counts[i] = counts[i] + extra
            surplus = surplus - extra
    return np.array(counts)


def centred(rng, dims, scale, reach, pieces=(), kind=jnp.bfloat16):
    result = scale * jax.random.normal(rng, dims, jnp.float32)
    if pieces:
        result = result * shard_levels(rng, dims, pieces, -0.22, 0.18)
    return jnp.clip(result, -reach, reach).astype(kind)


def setup_inputs(seed: int = 0) -> dict:
    keys = jax.random.split(jax.random.key(seed), 9)
    source = centred(keys[0], (SOUNDS, 6, NXF, NY * NZ), 1.0, 6.0, ((0, 32), (2, 4)), jnp.float32)
    adjoint = centred(keys[1], (SOUNDS, NFREQ, 6, NXF, NY * NZ), 0.5, 3.0, ((0, 32), (1, 4), (3, 4)), jnp.float32)
    omegas = jnp.clip(jnp.exp(math.log(8.0) - 2.7725887 * jax.random.uniform(keys[2], (NFREQ,), jnp.float32) ** shard_levels(keys[2], (NFREQ,), ((0, 4),), -0.2, 0.2)), 0.5, 8.0)
    background = jnp.clip(jnp.exp(jax.random.uniform(keys[3], (3,), jnp.float32, math.log(0.1), math.log(1.0))), 0.1, 1.0)
    conductivity = jnp.clip(jnp.exp(math.log(5.0) - 4.6051702 * jax.random.uniform(keys[4], (GBLK, 384), jnp.float32) ** shard_levels(keys[4], (GBLK, 384), ((0, 128),), -0.2, 0.2)), 0.05, 5.0)
    block_owner_keys = jax.random.split(jax.random.fold_in(keys[5], 1), SOUNDS * FBLK // FB_DEV)
    block_owner_turns = jax.random.permutation(jax.random.fold_in(keys[5], 3), SOUNDS * FBLK // FB_DEV)
    block_owner = jax.vmap(lambda own, number: deal_out(jax.random.fold_in(keys[5], 2), own, number, FB_DEV, N_SND * N_MESH, 1, CAP, 2))(block_owner_keys, block_owner_turns).reshape((SOUNDS, FBLK, 1))
    block_local = with_ends(jax.random.randint(keys[6], (SOUNDS, FBLK), 0, GB_DEV), jax.random.fold_in(keys[6], 1), 0, GB_DEV - 1).astype(jnp.int32)
    block_count = with_ends(jax.random.randint(keys[7], (SOUNDS,), FBLK // 2, FBLK + 1), jax.random.fold_in(keys[7], 1), FBLK // 2, FBLK).astype(jnp.int32)
    return {"source": source, "adjoint": adjoint, "omegas": omegas, "background": background, "conductivity": conductivity, "block_owner": block_owner, "block_local": block_local, "block_count": block_count}


RELAX_FACTOR = 0.5


def ahead_cells(values, offset, keep):
    padded = jnp.pad(values, [(0, 0)] * (values.ndim - 1) + [(0, offset)])
    return padded[..., offset:] * keep


def behind_cells(values, offset, keep):
    padded = jnp.pad(values, [(0, 0)] * (values.ndim - 1) + [(offset, 0)])
    return padded[..., :-offset] * keep


def cell_masks(count_second, count_third):
    cell_index = jnp.arange(count_second * count_third, dtype=jnp.int32)
    third_coord = cell_index % count_third
    second_coord = cell_index // count_third
    third_up = (third_coord < count_third - 1).astype(jnp.float32)
    third_down = (third_coord > 0).astype(jnp.float32)
    second_up = (second_coord < count_second - 1).astype(jnp.float32)
    second_down = (second_coord > 0).astype(jnp.float32)
    return third_up, third_down, second_up, second_down


def curl_curl(padded_field, keep_first, edge_masks, count_third):
    third_up, third_down, second_up, second_down = edge_masks
    components = padded_field.reshape(2, 3, padded_field.shape[1], padded_field.shape[2])
    along_first = components[:, 0]
    along_second = components[:, 1]
    along_third = components[:, 2]

    def step_first(values):
        return values[:, 1:] - values[:, :-1]

    def step_second(values):
        return ahead_cells(values[:, :-1], count_third, second_up) - values[:, :-1]

    def step_third(values):
        return ahead_cells(values[:, :-1], 1, third_up) - values[:, :-1]

    curl_first = step_second(along_third) - step_third(along_second)
    curl_second = step_third(along_first) - step_first(along_third)
    curl_third = step_first(along_second) - step_second(along_first)
    row_count = curl_first.shape[1]
    first_row = (jnp.arange(row_count) == 0)[None, :, None]
    row_scale = jnp.where(first_row, keep_first, 1.0).astype(jnp.float32)
    curl_first = curl_first * row_scale
    curl_second = curl_second * row_scale
    curl_third = curl_third * row_scale

    def back_first(values):
        return values[:, :-1] - values[:, 1:]

    def back_second(values):
        return behind_cells(values[:, 1:], count_third, second_down) - values[:, 1:]

    def back_third(values):
        return behind_cells(values[:, 1:], 1, third_down) - values[:, 1:]

    image_first = back_third(curl_second) - back_second(curl_third)
    image_second = back_first(curl_third) - back_third(curl_first)
    image_third = back_second(curl_first) - back_first(curl_second)
    return jnp.stack([image_first, image_second, image_third], axis=1)


def relax_step(field_now, forcing, applied, weights):
    field_real = field_now[:3]
    field_imag = field_now[3:]
    resid_real = forcing[:3] - applied[:3] + weights * field_imag
    resid_imag = forcing[3:] - applied[3:] - weights * field_real
    denominator = 16.0 + weights * weights
    new_real = field_real + RELAX_FACTOR * (4.0 * resid_real + weights * resid_imag) / denominator
    new_imag = field_imag + RELAX_FACTOR * (4.0 * resid_imag - weights * resid_real) / denominator
    return jnp.concatenate([new_real, new_imag], axis=0)


def reference(source, adjoint, omegas, background, conductivity, block_owner, block_local, block_count):
    edge_masks = cell_masks(NY, NZ)
    base_row = jnp.repeat(background, 128)
    block_total = NXF * NY * NZ // 128
    plane_cells = NY * NZ

    def per_sounding(gradient, inputs):
        forcing, adjoint_all, owner_ids, local_ids, live_count = inputs
        global_ids = (owner_ids[:, 0] * GB_DEV + local_ids).astype(jnp.int32)
        live_flags = jnp.arange(block_total, dtype=jnp.int32) < live_count
        blocks = jnp.where(live_flags[:, None], jnp.take(conductivity, global_ids, axis=0), base_row[None, :])
        sigma_field = blocks.reshape(block_total, 3, 128).transpose(1, 0, 2).reshape(3, NXF, plane_cells)
        fields = []
        for freq_index in range(NFREQ):
            weights = omegas[freq_index] * sigma_field
            field_now = jnp.zeros_like(forcing)
            for step_index in range(ITERS):
                if step_index == 0:
                    applied = jnp.zeros_like(forcing)
                else:
                    padded = jnp.pad(field_now, ((0, 0), (1, 1), (0, 0)))
                    applied = curl_curl(padded, 0.0, edge_masks, NZ).reshape(6, NXF, plane_cells)
                field_now = relax_step(field_now, forcing, applied, weights)
            adjoint_field = adjoint_all[freq_index]
            sensitivity = omegas[freq_index] * (adjoint_field[:3] * field_now[3:] - adjoint_field[3:] * field_now[:3])
            grad_blocks = sensitivity.reshape(3, block_total, 128).transpose(1, 0, 2).reshape(block_total, 384)
            grad_blocks = jnp.where(live_flags[:, None], grad_blocks, 0.0)
            gradient = gradient + jax.ops.segment_sum(grad_blocks, global_ids, num_segments=GBLK)
            fields.append(field_now)
        return gradient, jnp.stack(fields)

    gradient, fields = lax.scan(per_sounding, jnp.zeros((GBLK, 384), jnp.float32), (source, adjoint, block_owner, block_local, block_count))
    return fields, gradient
```

```python
import functools
import jax
import jax.numpy as jnp
from jax import lax
from jax.sharding import PartitionSpec as P
from jax.experimental import pallas as pl
from jax.experimental.pallas import tpu as pltpu

NZ = 48
ITERS = 4
ROWS = 8
BLOCKS = 192
LAYER = 24
HALO = ITERS - 1
EXT = ROWS + 2 * HALO
OWN0 = HALO * LAYER
HSZ = HALO * LAYER
ESZ = EXT * LAYER
N_OWN = 128
N_MESH = 4
N_FREQ = 4
PER = BLOCKS // N_FREQ
LOCAL = 64
F32 = jnp.float32
BF16 = jnp.bfloat16
I32 = jnp.int32
MESH = pl.DeviceIdType.MESH


def iota(shape, dim):
    return lax.broadcasted_iota(I32, shape, dim)


def onehot(mask):
    return jnp.where(mask, 1.0, 0.0).astype(BF16)


def pick(rows, values):
    high = values.astype(BF16)
    low = (values - high.astype(F32)).astype(BF16)
    dot = functools.partial(jnp.dot, preferred_element_type=F32)
    return dot(rows, high) + dot(rows, low)


def kernel(
    omegas, background, count, owner_in, local_in, cond, source_hbm, adjoint_hbm,
    field_hbm, grad_out,
    src_raw, adj_raw, src, adj, sig, fld, crl,
    ask, wanted, replies, fetched, shared, grads, summed, slots, arrived, partial_,
    in_sem, out_sem, ask_s, ask_r, rep_s, rep_r, sh_s, sh_r, hs_s, hs_r, hw_s, hw_r,
    rs_s, rs_r, gr_s, gr_r, ps_s, ps_r,
):
    s, f, m = lax.axis_index("snd"), lax.axis_index("freq"), lax.axis_index("mesh")
    z, core = s // 2, s % 2
    me = s * N_MESH + m

    def each_peer(act):
        def group(dz, with_self):
            for dm in (2, 1, 3, 0):
                for flip in (0, 1):
                    if with_self and dm == 0 and flip == 0:
                        continue
                    act(((z + dz) % 16) * 2 + (core if flip == 0 else 1 - core), (m + dm) % N_MESH)

        def body(i, carry):
            group(8 + (1 - 2 * (i % 2)) * ((i + 1) // 2), False)
            return carry

        lax.fori_loop(0, 15, body, 0)
        group(0, True)

    barrier = pltpu.get_barrier_semaphore()

    def greet(ps, pm):
        pl.semaphore_signal(barrier, inc=1, device_id={"snd": ps, "mesh": pm}, device_id_type=MESH)

    each_peer(greet)
    for k in range(1, N_FREQ):
        pl.semaphore_signal(
            barrier, inc=1, device_id={"freq": (f + k) % N_FREQ}, device_id_type=MESH
        )

    def remote(a, b, ss, rs, **to):
        return pltpu.make_async_remote_copy(
            src_ref=a, dst_ref=b, send_sem=ss, recv_sem=rs, device_id=to, device_id_type=MESH
        )

    def wait(ref, sem):
        pltpu.make_async_copy(ref, ref, sem).wait()

    load_src = pltpu.make_async_copy(source_hbm.at[0], src_raw, in_sem.at[0])
    load_adj = pltpu.make_async_copy(adjoint_hbm.at[0, 0], adj_raw, in_sem.at[1])
    load_src.start()
    load_adj.start()

    eye = iota((BLOCKS, BLOCKS), 0) == iota((BLOCKS, BLOCKS), 1)

    def to_col(row):
        return jnp.sum(jnp.where(eye, row, 0), axis=1, keepdims=True)

    owner_row = owner_in[...]
    owner_col = to_col(owner_row)
    local_col = to_col(local_in[...])
    key_row = owner_row * 256 + iota((1, BLOCKS), 1)
    key_col = owner_col * 256 + iota((BLOCKS, 1), 0)
    pos_row = jnp.sum(jnp.where(key_col < key_row, 1, 0), axis=0, keepdims=True)
    pos_col = jnp.sum(jnp.where(key_row < key_col, 1, 0), axis=1, keepdims=True)
    place_row = (pos_row % N_FREQ) * PER + pos_row // N_FREQ
    place_col = (pos_col % N_FREQ) * PER + pos_col // N_FREQ
    owners = iota((1, N_OWN), 1)
    mine = (owner_col == owners) & (pos_col % N_FREQ == f)
    ask[...] = jnp.sum(jnp.where(mine, local_col + 1, 0), axis=0, keepdims=True)

    def spread(raw, out, first):
        for c in range(6):
            for k in range(LAYER):
                out[c, pl.ds(first + k, ROWS, stride=LAYER), :] = raw[c, :, k * 128 : (k + 1) * 128]

    load_src.wait()
    spread(src_raw, src, OWN0)

    pl.semaphore_wait(barrier, N_OWN - 1 + N_FREQ - 1)

    wanted[pl.ds(me, 1), :] = ask[...]
    each_peer(
        lambda ps, pm: remote(
            ask, wanted.at[pl.ds(me, 1)], ask_s, ask_r, snd=ps, mesh=pm
        ).start()
    )

    up, down = (m + 1) % N_MESH, (m + 3) % N_MESH

    def trade_layers(ref, ss, rs):
        remote(
            ref.at[:, pl.ds(OWN0 + BLOCKS - HSZ, HSZ)], ref.at[:, pl.ds(0, HSZ)], ss.at[0], rs.at[0], mesh=up
        ).start()
        remote(
            ref.at[:, pl.ds(OWN0, HSZ)], ref.at[:, pl.ds(OWN0 + BLOCKS, HSZ)], ss.at[1], rs.at[1], mesh=down
        ).start()

    def layers_in(ref, rs):
        wait(ref.at[:, pl.ds(0, HSZ)], rs.at[0])
        wait(ref.at[:, pl.ds(OWN0 + BLOCKS, HSZ)], rs.at[1])

    def layers_out(ref, ss):
        wait(ref.at[:, pl.ds(OWN0 + BLOCKS - HSZ, HSZ)], ss.at[0])
        wait(ref.at[:, pl.ds(OWN0, HSZ)], ss.at[1])

    trade_layers(src, hs_s, hs_r)

    load_adj.wait()
    spread(adj_raw, adj, 0)

    less_row = jnp.sum(jnp.where(owner_col < owners, 1, 0), axis=0, keepdims=True)
    many_row = jnp.sum(jnp.where(owner_col == owners, 1, 0), axis=0, keepdims=True)
    owners_c = iota((N_OWN, 1), 0)
    less_col = jnp.sum(jnp.where(owner_row < owners_c, 1, 0), axis=1, keepdims=True)
    many_col = jnp.sum(jnp.where(owner_row == owners_c, 1, 0), axis=1, keepdims=True)
    at_col = iota((PER, 1), 0) * N_FREQ + f
    at_row = iota((1, PER), 1) * N_FREQ + f
    squeeze = onehot((at_col >= less_row) & (at_col < less_row + many_row))
    widen = onehot((at_row >= less_col) & (at_row < less_col + many_col))
    unsort = onehot(place_col == iota((1, BLOCKS), 1))
    resort = onehot(iota((BLOCKS, 1), 0) == place_row)

    wait(wanted.at[pl.ds(0, N_OWN - 1)], ask_r)
    asked = jnp.sum(
        jnp.where(iota((N_OWN, N_OWN), 1) == me, wanted[...], 0), axis=1, keepdims=True
    )
    asked_row = jnp.sum(
        jnp.where(iota((N_OWN, N_OWN), 0) == iota((N_OWN, N_OWN), 1), asked, 0), axis=0, keepdims=True
    )
    look = onehot(asked - 1 == iota((1, LOCAL), 1))
    answer = pick(look, cond[...])
    for c in range(3):
        replies[c] = answer[:, c * 128 : (c + 1) * 128]
    each_peer(
        lambda ps, pm: remote(
            replies.at[:, pl.ds(ps * N_MESH + pm, 1)], fetched.at[:, pl.ds(me, 1)], rep_s, rep_r,
            snd=ps, mesh=pm,
        ).start()
    )
    fetched[:, pl.ds(me, 1), :] = replies[:, pl.ds(me, 1), :]
    wait(fetched.at[:, pl.ds(0, N_OWN - 1)], rep_r)

    own_part = pl.ds(pl.multiple_of(f * PER, 8), PER)
    for c in range(3):
        shared[c, own_part, :] = pick(squeeze, fetched[c])
    for k in range(1, N_FREQ):
        remote(
            shared.at[:, own_part], shared.at[:, own_part], sh_s, sh_r, freq=(f + k) % N_FREQ
        ).start()
    wait(shared.at[:, pl.ds(0, BLOCKS - PER)], sh_r)

    live = m * BLOCKS + iota((BLOCKS, 1), 0) < count[0]
    for c in range(3):
        sig[c, pl.ds(OWN0, BLOCKS), :] = jnp.where(live, pick(unsort, shared[c]), background[c])
    trade_layers(sig, hw_s, hw_r)
    layers_in(src, hs_r)
    layers_in(sig, hw_r)

    omega = omegas[0]
    low_keep = jnp.where(m > 0, 1.0, 0.0)
    high_keep = jnp.where(m < N_MESH - 1, 1.0, 0.0)
    shape = (LAYER, 128)
    lane = iota(shape, 1)
    cell = iota(shape, 0) * 128 + lane
    third = cell % NZ

    def shifted(x, by, axis_roll, wrap, zero):
        r = pltpu.roll(x, by % 128, 1)
        r = jnp.where(wrap, pltpu.roll(r, axis_roll, 0), r)
        return jnp.where(zero, 0.0, r)

    def sy(x):
        return shifted(x, -NZ, LAYER - 1, lane >= 128 - NZ, cell >= LAYER * 128 - NZ)

    def sz(x):
        return shifted(x, -1, LAYER - 1, lane == 127, third == NZ - 1)

    def by(x):
        return shifted(x, NZ, 1, lane < NZ, cell < NZ)

    def bz(x):
        return shifted(x, 1, 1, lane == 0, third == 0)

    def at(i):
        return pl.ds(pl.multiple_of(i * LAYER, 8), LAYER)

    def keep_src(i):
        return jnp.where(i < HALO, low_keep, jnp.where(i >= HALO + ROWS, high_keep, 1.0))

    def relax(i, sr, si, er, ei, w):
        rr, ri = sr, si
        if er is not None:
            rr = rr + w * ei
            ri = ri - w * er
        scale = 0.5 / (16.0 + w * w)
        nr = scale * (4.0 * rr + w * ri)
        ni = scale * (4.0 * ri - w * rr)
        if er is not None:
            nr, ni = er + nr, ei + ni
        return nr, ni

    def first(i, carry):
        keep = keep_src(i)
        for c in range(3):
            w = omega * sig[c, at(i), :]
            nr, ni = relax(i, src[c, at(i), :] * keep, src[c + 3, at(i), :] * keep, None, None, w)
            fld[c, at(i), :] = nr
            fld[c + 3, at(i), :] = ni
        return carry

    lax.fori_loop(0, EXT, first, 0)

    for it in range(1, ITERS):
        lo, hi = it, EXT - it

        def curl(i, carry):
            keep = jnp.where(i < HALO, low_keep, 1.0)
            for p in (0, 3):
                ex, ey, ez = (fld[p + c, at(i), :] for c in range(3))
                ny, nz = fld[p + 1, at(i + 1), :], fld[p + 2, at(i + 1), :]
                crl[p, at(i), :] = ((sy(ez) - ez) - (sz(ey) - ey)) * keep
                crl[p + 1, at(i), :] = ((sz(ex) - ex) - (nz - ez)) * keep
                crl[p + 2, at(i), :] = ((ny - ey) - (sy(ex) - ex)) * keep
            return carry

        lax.fori_loop(lo - 1, hi, curl, 0)

        def update(i, carry):
            keep = jnp.where(i >= HALO + ROWS, high_keep, 1.0)
            ksrc = keep_src(i)
            image = []
            for p in (0, 3):
                hx, hy, hz = (crl[p + c, at(i), :] for c in range(3))
                py, pz = crl[p + 1, at(i - 1), :], crl[p + 2, at(i - 1), :]
                image.append((bz(hy) - hy) - (by(hz) - hz))
                image.append((pz - hz) - (bz(hx) - hx))
                image.append((by(hx) - hx) - (py - hy))
            for c in range(3):
                w = omega * sig[c, at(i), :]
                er, ei = fld[c, at(i), :], fld[c + 3, at(i), :]
                nr, ni = relax(
                    i,
                    src[c, at(i), :] * ksrc - image[c] * keep,
                    src[c + 3, at(i), :] * ksrc - image[c + 3] * keep,
                    er, ei, w,
                )
                fld[c, at(i), :] = nr
                fld[c + 3, at(i), :] = ni
            return carry

        lax.fori_loop(lo, hi, update, 0)

    own = pl.ds(OWN0, BLOCKS)
    for c in range(3):
        sens = omega * (adj[c] * fld[c + 3, own, :] - adj[c + 3] * fld[c, own, :])
        grads[c] = pick(resort, jnp.where(live, sens, 0.0))
    for k in range(1, N_FREQ):
        to = (f + k) % N_FREQ
        remote(
            grads.at[:, pl.ds(pl.multiple_of(to * PER, 8), PER)], summed.at[f], rs_s, rs_r, freq=to
        ).start()
    summed[f] = grads[:, own_part, :]

    for c in range(6):
        for k in range(LAYER):
            src_raw[c, :, k * 128 : (k + 1) * 128] = fld[c, pl.ds(OWN0 + k, ROWS, stride=LAYER), :]
    store = pltpu.make_async_copy(src_raw, field_hbm.at[0, 0], out_sem)
    store.start()

    wait(summed.at[pl.ds(0, N_FREQ - 1)], rs_r)
    for c in range(3):
        total = (summed[0, c] + summed[1, c]) + (summed[2, c] + summed[3, c])
        slots[c] = pick(widen, total)
    each_peer(
        lambda ps, pm: remote(
            slots.at[:, pl.ds(ps * N_MESH + pm, 1)], arrived.at[:, pl.ds(me, 1)], gr_s, gr_r,
            snd=ps, mesh=pm,
        ).start()
    )
    arrived[:, pl.ds(me, 1), :] = slots[:, pl.ds(me, 1), :]
    collect = onehot(asked_row - 1 == iota((LOCAL, 1), 0))
    wait(arrived.at[:, pl.ds(0, N_OWN - 1)], gr_r)
    for c in range(3):
        partial_[f, c] = pick(collect, arrived[c])
    for k in range(1, N_FREQ):
        remote(partial_.at[f], partial_.at[f], ps_s, ps_r, freq=(f + k) % N_FREQ).start()
    wait(partial_.at[pl.ds(0, N_FREQ - 1)], ps_r)
    for c in range(3):
        grad_out[:, c * 128 : (c + 1) * 128] = (partial_[0, c] + partial_[1, c]) + (
            partial_[2, c] + partial_[3, c]
        )

    wait(wanted.at[pl.ds(0, N_OWN - 1)], ask_s)
    wait(fetched.at[:, pl.ds(0, N_OWN - 1)], rep_s)
    wait(shared.at[:, pl.ds(0, BLOCKS - PER)], sh_s)
    layers_out(src, hs_s)
    layers_out(sig, hw_s)
    wait(summed.at[pl.ds(0, N_FREQ - 1)], rs_s)
    wait(arrived.at[:, pl.ds(0, N_OWN - 1)], gr_s)
    wait(partial_.at[pl.ds(0, N_FREQ - 1)], ps_s)
    store.wait()


def on_device(
    source, adjoint, omegas, background, conductivity, block_owner, block_local, block_count
):
    smem = pl.BlockSpec(memory_space=pltpu.SMEM)
    vmem = pl.BlockSpec(memory_space=pltpu.VMEM)
    hbm = pl.BlockSpec(memory_space=pl.ANY)
    buf = lambda *shape: pltpu.VMEM(shape, F32)
    dma = pltpu.SemaphoreType.DMA
    return pl.pallas_call(
        kernel,
        out_shape=(
            jax.ShapeDtypeStruct(adjoint.shape, F32),
            jax.ShapeDtypeStruct(conductivity.shape, F32),
        ),
        in_specs=[smem, smem, smem, vmem, vmem, vmem, hbm, hbm],
        out_specs=(hbm, vmem),
        scratch_shapes=[
            buf(6, ROWS, LAYER * 128),
            buf(6, ROWS, LAYER * 128),
            buf(6, ESZ, 128),
            buf(6, BLOCKS, 128),
            buf(3, ESZ, 128),
            buf(6, ESZ, 128),
            buf(6, ESZ, 128),
            pltpu.VMEM((1, N_OWN), I32),
            pltpu.VMEM((N_OWN, N_OWN), I32),
            buf(3, N_OWN, 128),
            buf(3, N_OWN, 128),
            buf(3, BLOCKS, 128),
            buf(3, BLOCKS, 128),
            buf(N_FREQ, 3, PER, 128),
            buf(3, N_OWN, 128),
            buf(3, N_OWN, 128),
            buf(N_FREQ, 3, LOCAL, 128),
            dma((2,)),
            dma,
        ]
        + [dma] * 6
        + [dma((2,))] * 4
        + [dma] * 6,
        compiler_params=pltpu.CompilerParams(
            collective_id=0, has_side_effects=True, vmem_limit_bytes=40 << 20
        ),
    )(
        omegas, background, block_count, block_owner.reshape(1, BLOCKS), block_local,
        conductivity, source, adjoint,
    )


def solution(mesh):
    return jax.shard_map(
        on_device,
        mesh=mesh,
        in_specs=(
            P("snd", None, "mesh", None),
            P("snd", "freq", None, "mesh", None),
            P("freq"),
            P(),
            P(("snd", "mesh"), None),
            P("snd", "mesh", None),
            P("snd", "mesh"),
            P("snd"),
        ),
        out_specs=(P("snd", "freq", None, "mesh", None), P(("snd", "mesh"), None)),
        check_vma=False,
    )
```

```python
import functools
import jax
import jax.numpy as jnp
from jax import lax
from jax.sharding import PartitionSpec as P
from jax.experimental import pallas as pl
from jax.experimental.pallas import tpu as pltpu

NZ = 48
ITERS = 4
ROWS = 8
BLOCKS = 192
LAYER = 24
HALO = ITERS - 1
EXT = ROWS + 2 * HALO
OWN0 = HALO * LAYER
HSZ = HALO * LAYER
ESZ = EXT * LAYER
N_OWN = 128
N_MESH = 4
N_FREQ = 4
PER = BLOCKS // N_FREQ
LOCAL = 64
F32 = jnp.float32
BF16 = jnp.bfloat16
I32 = jnp.int32
MESH = pl.DeviceIdType.MESH
CHUNKS = ((0, 2), (2, 1))


def iota(shape, dim):
    return lax.broadcasted_iota(I32, shape, dim)


def onehot(mask):
    return jnp.where(mask, 1.0, 0.0).astype(BF16)


def pick(rows, values):
    high = values.astype(BF16)
    low = (values - high.astype(F32)).astype(BF16)
    dot = functools.partial(jnp.dot, preferred_element_type=F32)
    return dot(rows, high) + dot(rows, low)


def kernel(
    omegas_hbm, background_hbm, count_hbm, owner_hbm, local_hbm, cond_hbm, source_hbm, adjoint_hbm,
    field_hbm, grad_hbm,
    omegas, background, count, owner_in, local_in, cond, grad_out, src_raw, adj_raw, src, adj, sig, wgt, fld, crl,
    ask, wanted, replies, fetched, shared, grads, summed, slots, arrived, partial_,
    in_sem, out_sem, ask_s, ask_r, rep_s, rep_r, sh_s, sh_r, hs_s, hs_r, hw_s, hw_r,
    rs_s, rs_r, gr_s, gr_r, ps_s, ps_r,
):
    s, f, m = lax.axis_index("snd"), lax.axis_index("freq"), lax.axis_index("mesh")
    z, core = s // 2, s % 2
    me = s * N_MESH + m

    def each_peer(act):
        def group(dz, with_self):
            for dm in (2, 1, 3, 0):
                for flip in (0, 1):
                    if with_self and dm == 0 and flip == 0:
                        continue
                    act(((z + dz) % 16) * 2 + (core if flip == 0 else 1 - core), (m + dm) % N_MESH)

        def body(i, carry):
            group(8 + (1 - 2 * (i % 2)) * ((i + 1) // 2), False)
            return carry

        lax.fori_loop(0, 15, body, 0)
        group(0, True)

    barrier = pltpu.get_barrier_semaphore()

    def greet(ps, pm):
        pl.semaphore_signal(barrier, inc=1, device_id={"snd": ps, "mesh": pm}, device_id_type=MESH)

    each_peer(greet)
    for k in range(1, N_FREQ):
        pl.semaphore_signal(
            barrier, inc=1, device_id={"freq": (f + k) % N_FREQ}, device_id_type=MESH
        )

    def remote(a, b, ss, rs, **to):
        return pltpu.make_async_remote_copy(
            src_ref=a, dst_ref=b, send_sem=ss, recv_sem=rs, device_id=to, device_id_type=MESH
        )

    def wait(ref, sem):
        pltpu.make_async_copy(ref, ref, sem).wait()

    load_src = pltpu.make_async_copy(source_hbm.at[0], src_raw, in_sem.at[0])
    load_adj = pltpu.make_async_copy(adjoint_hbm.at[0, 0], adj_raw, in_sem.at[1])
    small = [
        pltpu.make_async_copy(a, b, in_sem.at[2 + i])
        for i, (a, b) in enumerate(
            (
                (owner_hbm, owner_in),
                (local_hbm, local_in),
                (cond_hbm, cond),
                (omegas_hbm, omegas),
                (background_hbm, background),
                (count_hbm, count),
            )
        )
    ]
    for copy in small:
        copy.start()
    load_src.start()
    load_adj.start()
    for copy in small:
        copy.wait()

    eye = iota((BLOCKS, BLOCKS), 0) == iota((BLOCKS, BLOCKS), 1)

    def to_col(row):
        return jnp.sum(jnp.where(eye, row, 0), axis=1, keepdims=True)

    owner_row = owner_in[...]
    owner_col = to_col(owner_row)
    local_col = to_col(local_in[...])
    key_row = owner_row * 256 + iota((1, BLOCKS), 1)
    key_col = owner_col * 256 + iota((BLOCKS, 1), 0)
    pos_row = jnp.sum(jnp.where(key_col < key_row, 1, 0), axis=0, keepdims=True)
    pos_col = jnp.sum(jnp.where(key_row < key_col, 1, 0), axis=1, keepdims=True)
    place_row = (pos_row % N_FREQ) * PER + pos_row // N_FREQ
    place_col = (pos_col % N_FREQ) * PER + pos_col // N_FREQ
    owners = iota((1, N_OWN), 1)
    mine = (owner_col == owners) & (pos_col % N_FREQ == f)
    ask[...] = jnp.sum(jnp.where(mine, local_col + 1, 0), axis=0, keepdims=True)

    def spread(raw, out, first):
        for c in range(6):
            for k in range(LAYER):
                out[c, pl.ds(first + k, ROWS, stride=LAYER), :] = raw[c, :, k * 128 : (k + 1) * 128]

    load_src.wait()
    spread(src_raw, src, OWN0)

    pl.semaphore_wait(barrier, N_OWN - 1 + N_FREQ - 1)

    wanted[pl.ds(me, 1), :] = ask[...]
    each_peer(
        lambda ps, pm: remote(
            ask, wanted.at[pl.ds(me, 1)], ask_s, ask_r, snd=ps, mesh=pm
        ).start()
    )

    up, down = (m + 1) % N_MESH, (m + 3) % N_MESH

    def trade_layers(ref, ss, rs, first, number):
        part = pl.ds(first, number)
        remote(
            ref.at[part, pl.ds(OWN0 + BLOCKS - HSZ, HSZ)], ref.at[part, pl.ds(0, HSZ)],
            ss.at[0], rs.at[0], mesh=up,
        ).start()
        remote(
            ref.at[part, pl.ds(OWN0, HSZ)], ref.at[part, pl.ds(OWN0 + BLOCKS, HSZ)],
            ss.at[1], rs.at[1], mesh=down,
        ).start()

    def layers_in(ref, rs, first, number):
        part = pl.ds(first, number)
        wait(ref.at[part, pl.ds(0, HSZ)], rs.at[0])
        wait(ref.at[part, pl.ds(OWN0 + BLOCKS, HSZ)], rs.at[1])

    def layers_out(ref, ss, first, number):
        part = pl.ds(first, number)
        wait(ref.at[part, pl.ds(OWN0 + BLOCKS - HSZ, HSZ)], ss.at[0])
        wait(ref.at[part, pl.ds(OWN0, HSZ)], ss.at[1])

    trade_layers(src, hs_s, hs_r, 0, 6)

    load_adj.wait()
    spread(adj_raw, adj, 0)

    less_row = jnp.sum(jnp.where(owner_col < owners, 1, 0), axis=0, keepdims=True)
    many_row = jnp.sum(jnp.where(owner_col == owners, 1, 0), axis=0, keepdims=True)
    owners_c = iota((N_OWN, 1), 0)
    less_col = jnp.sum(jnp.where(owner_row < owners_c, 1, 0), axis=1, keepdims=True)
    many_col = jnp.sum(jnp.where(owner_row == owners_c, 1, 0), axis=1, keepdims=True)
    at_col = iota((PER, 1), 0) * N_FREQ + f
    at_row = iota((1, PER), 1) * N_FREQ + f
    squeeze = onehot((at_col >= less_row) & (at_col < less_row + many_row))
    widen = onehot((at_row >= less_col) & (at_row < less_col + many_col))
    unsort = onehot(place_col == iota((1, BLOCKS), 1))
    resort = onehot(iota((BLOCKS, 1), 0) == place_row)

    low_keep = jnp.where(m > 0, 1.0, 0.0)
    high_keep = jnp.where(m < N_MESH - 1, 1.0, 0.0)
    layers_in(src, hs_r, 0, 6)
    for c in range(6):
        src[c, 0:OWN0, :] = src[c, 0:OWN0, :] * low_keep
        src[c, OWN0 + BLOCKS : ESZ, :] = src[c, OWN0 + BLOCKS : ESZ, :] * high_keep

    wait(wanted.at[pl.ds(0, N_OWN - 1)], ask_r)
    asked = jnp.sum(
        jnp.where(iota((N_OWN, N_OWN), 1) == me, wanted[...], 0), axis=1, keepdims=True
    )
    look = onehot(asked - 1 == iota((1, LOCAL), 1))

    def scatter_rows(a, b, ss, rs, first, number):
        part = pl.ds(first, number)
        each_peer(
            lambda ps, pm: remote(
                a.at[part, pl.ds(ps * N_MESH + pm, 1)], b.at[part, pl.ds(me, 1)], ss, rs,
                snd=ps, mesh=pm,
            ).start()
        )
        b[part, pl.ds(me, 1), :] = a[part, pl.ds(me, 1), :]

    for k, (first, number) in enumerate(CHUNKS):
        for c in range(first, first + number):
            replies[c] = pick(look, cond[:, c * 128 : (c + 1) * 128])
        scatter_rows(replies, fetched, rep_s.at[k], rep_r.at[k], first, number)
    asked_row = jnp.sum(
        jnp.where(iota((N_OWN, N_OWN), 0) == iota((N_OWN, N_OWN), 1), asked, 0), axis=0, keepdims=True
    )

    own_part = pl.ds(pl.multiple_of(f * PER, 8), PER)
    for k, (first, number) in enumerate(CHUNKS):
        part = pl.ds(first, number)
        wait(fetched.at[part, pl.ds(0, N_OWN - 1)], rep_r.at[k])
        for c in range(first, first + number):
            shared[c, own_part, :] = pick(squeeze, fetched[c])
        for to in range(1, N_FREQ):
            remote(
                shared.at[part, own_part], shared.at[part, own_part], sh_s.at[k], sh_r.at[k],
                freq=(f + to) % N_FREQ,
            ).start()

    live = m * BLOCKS + iota((BLOCKS, 1), 0) < count[0]
    for k, (first, number) in enumerate(CHUNKS):
        wait(shared.at[pl.ds(first, number), pl.ds(0, BLOCKS - PER)], sh_r.at[k])
        for c in range(first, first + number):
            sig[c, pl.ds(OWN0, BLOCKS), :] = jnp.where(live, pick(unsort, shared[c]), background[c])
        trade_layers(sig, hw_s.at[k], hw_r.at[k], first, number)

    omega = omegas[0]
    shape = (LAYER, 128)
    lane = iota(shape, 1)
    cell = iota(shape, 0) * 128 + lane
    third = cell % NZ
    y_last, z_last = cell >= LAYER * 128 - NZ, third == NZ - 1
    y_first, z_first = cell < NZ, third == 0

    def at(i, offset=0):
        start = i * LAYER
        return pl.ds(pl.multiple_of(start, 8) if offset == 0 else start + offset, LAYER)

    def sy(x, after):
        return jnp.where(y_last, 0.0, pltpu.roll(jnp.where(lane < NZ, after, x), 128 - NZ, 1))

    def sz(x, after):
        return jnp.where(z_last, 0.0, pltpu.roll(jnp.where(lane < 1, after, x), 127, 1))

    def by(x, before):
        return jnp.where(y_first, 0.0, pltpu.roll(jnp.where(lane >= 128 - NZ, before, x), NZ, 1))

    def bz(x, before):
        return jnp.where(z_first, 0.0, pltpu.roll(jnp.where(lane >= 127, before, x), 1, 1))

    def begin(i):
        for c in range(3):
            w = omega * sig[c, at(i), :]
            scale = 0.5 / (16.0 + w * w)
            real, imag = 4.0 * scale, w * scale
            sr, si = src[c, at(i), :], src[c + 3, at(i), :]
            wgt[c, at(i), :] = w
            wgt[c + 3, at(i), :] = real
            wgt[c + 6, at(i), :] = imag
            fld[c, at(i), :] = real * sr + imag * si
            fld[c + 3, at(i), :] = real * si - imag * sr

    def curl(i, keep=None):
        for p in (0, 3):
            ex, ey, ez = (fld[p + c, at(i), :] for c in range(3))
            ax, ay, az = (fld[p + c, at(i, 1), :] for c in range(3))
            ny, nz = fld[p + 1, at(i + 1), :], fld[p + 2, at(i + 1), :]
            hx = (sy(ez, az) - ez) - (sz(ey, ay) - ey)
            hy = (sz(ex, ax) - ex) - (nz - ez)
            hz = (ny - ey) - (sy(ex, ax) - ex)
            for c, h in enumerate((hx, hy, hz)):
                crl[p + c, at(i), :] = h if keep is None else h * keep

    def update(i, keep=None):
        image = []
        for p in (0, 3):
            hx, hy, hz = (crl[p + c, at(i), :] for c in range(3))
            bx, bhy, bhz = (crl[p + c, at(i, -1), :] for c in range(3))
            py, pz = crl[p + 1, at(i - 1), :], crl[p + 2, at(i - 1), :]
            image.append((bz(hy, bhy) - hy) - (by(hz, bhz) - hz))
            image.append((pz - hz) - (bz(hx, bx) - hx))
            image.append((by(hx, bx) - hx) - (py - hy))
        if keep is not None:
            image = [v * keep for v in image]
        for c in range(3):
            w, real, imag = (wgt[c + 3 * k, at(i), :] for k in range(3))
            er, ei = fld[c, at(i), :], fld[c + 3, at(i), :]
            rr = src[c, at(i), :] - image[c] + w * ei
            ri = src[c + 3, at(i), :] - image[c + 3] - w * er
            fld[c, at(i), :] = er + (real * rr + imag * ri)
            fld[c + 3, at(i), :] = ei + (real * ri - imag * rr)

    def loop(lo, hi, act):
        def body(i, carry):
            act(i)
            return carry

        lax.fori_loop(lo, hi, body, 0)

    top = HALO + ROWS
    loop(HALO, top, begin)
    for it in range(1, ITERS):
        loop(HALO + it - 1, top - it, curl)
        loop(HALO + it, top - it, update)

    for k, (first, number) in enumerate(CHUNKS):
        layers_in(sig, hw_r.at[k], first, number)

    def edge_begin(i):
        begin(i)
        begin(i + top)

    loop(0, HALO, edge_begin)
    for it in range(1, ITERS):

        def edge_curl(j):
            low = it - 1 + j
            curl(low, jnp.where(low < HALO, low_keep, 1.0))
            curl(top - it + j)

        def edge_update(j):
            high = top - it + j
            update(it + j)
            update(high, jnp.where(high >= top, high_keep, 1.0))

        loop(0, HALO, edge_curl)
        loop(0, HALO, edge_update)

    own = pl.ds(OWN0, BLOCKS)
    for k, (first, number) in enumerate(CHUNKS):
        part = pl.ds(first, number)
        for c in range(first, first + number):
            sens = omega * (adj[c] * fld[c + 3, own, :] - adj[c + 3] * fld[c, own, :])
            grads[c] = pick(resort, jnp.where(live, sens, 0.0))
        for to in range(1, N_FREQ):
            peer = (f + to) % N_FREQ
            remote(
                grads.at[part, pl.ds(pl.multiple_of(peer * PER, 8), PER)], summed.at[f, part],
                rs_s.at[k], rs_r.at[k], freq=peer,
            ).start()
        summed[f, part] = grads[part, own_part, :]

    collect = onehot(asked_row - 1 == iota((LOCAL, 1), 0))
    for k, (first, number) in enumerate(CHUNKS):
        wait(summed.at[pl.ds(0, N_FREQ - 1), pl.ds(first, number)], rs_r.at[k])
        for c in range(first, first + number):
            total = (summed[0, c] + summed[1, c]) + (summed[2, c] + summed[3, c])
            slots[c] = pick(widen, total)
        scatter_rows(slots, arrived, gr_s.at[k], gr_r.at[k], first, number)

    for c in range(6):
        for k in range(LAYER):
            src_raw[c, :, k * 128 : (k + 1) * 128] = fld[c, pl.ds(OWN0 + k, ROWS, stride=LAYER), :]
    store = pltpu.make_async_copy(src_raw, field_hbm.at[0, 0], out_sem.at[0])
    store.start()

    for k, (first, number) in enumerate(CHUNKS):
        part = pl.ds(first, number)
        wait(arrived.at[part, pl.ds(0, N_OWN - 1)], gr_r.at[k])
        for c in range(first, first + number):
            partial_[f, c] = pick(collect, arrived[c])
        for to in range(1, N_FREQ):
            remote(
                partial_.at[f, part], partial_.at[f, part], ps_s.at[k], ps_r.at[k],
                freq=(f + to) % N_FREQ,
            ).start()
    for k, (first, number) in enumerate(CHUNKS):
        wait(partial_.at[pl.ds(0, N_FREQ - 1), pl.ds(first, number)], ps_r.at[k])
        for c in range(first, first + number):
            grad_out[:, c * 128 : (c + 1) * 128] = (partial_[0, c] + partial_[1, c]) + (
                partial_[2, c] + partial_[3, c]
            )
    store_grad = pltpu.make_async_copy(grad_out, grad_hbm, out_sem.at[1])
    store_grad.start()

    wait(wanted.at[pl.ds(0, N_OWN - 1)], ask_s)
    layers_out(src, hs_s, 0, 6)
    for k, (first, number) in enumerate(CHUNKS):
        part = pl.ds(first, number)
        wait(fetched.at[part, pl.ds(0, N_OWN - 1)], rep_s.at[k])
        wait(shared.at[part, pl.ds(0, BLOCKS - PER)], sh_s.at[k])
        layers_out(sig, hw_s.at[k], first, number)
        wait(summed.at[pl.ds(0, N_FREQ - 1), part], rs_s.at[k])
        wait(arrived.at[part, pl.ds(0, N_OWN - 1)], gr_s.at[k])
        wait(partial_.at[pl.ds(0, N_FREQ - 1), part], ps_s.at[k])
    store.wait()
    store_grad.wait()


def settle(field, gradient, field_out, gradient_out, held, held_gradient, sem_in, sem_out):
    ways = [(field.at[0, 0, c], held.at[c], field_out.at[0, 0, c]) for c in range(6)]
    ways.append((gradient, held_gradient, gradient_out))
    loads = [pltpu.make_async_copy(a, b, sem_in.at[i]) for i, (a, b, _) in enumerate(ways)]
    stores = [pltpu.make_async_copy(b, c, sem_out.at[i]) for i, (_, b, c) in enumerate(ways)]
    for load in loads:
        load.start()
    for load, store in zip(loads, stores):
        load.wait()
        store.start()
    for store in stores:
        store.wait()


def on_device(
    source, adjoint, omegas, background, conductivity, block_owner, block_local, block_count
):
    hbm = pl.BlockSpec(memory_space=pltpu.HBM)
    buf = lambda *shape: pltpu.VMEM(shape, F32)
    dma = pltpu.SemaphoreType.DMA
    parts = len(CHUNKS)
    field, gradient = pl.pallas_call(
        kernel,
        out_shape=(
            jax.ShapeDtypeStruct(adjoint.shape, F32),
            jax.ShapeDtypeStruct(conductivity.shape, F32),
        ),
        in_specs=[hbm] * 8,
        out_specs=(hbm, hbm),
        scratch_shapes=[
            pltpu.SMEM((1,), F32),
            pltpu.SMEM((3,), F32),
            pltpu.SMEM((1,), I32),
            pltpu.VMEM((1, BLOCKS), I32),
            pltpu.VMEM((1, BLOCKS), I32),
            buf(LOCAL, 384),
            buf(LOCAL, 384),
            buf(6, ROWS, LAYER * 128),
            buf(6, ROWS, LAYER * 128),
            buf(6, ESZ, 128),
            buf(6, BLOCKS, 128),
            buf(3, ESZ, 128),
            buf(9, ESZ, 128),
            buf(6, ESZ, 128),
            buf(6, ESZ, 128),
            pltpu.VMEM((1, N_OWN), I32),
            pltpu.VMEM((N_OWN, N_OWN), I32),
            buf(3, N_OWN, 128),
            buf(3, N_OWN, 128),
            buf(3, BLOCKS, 128),
            buf(3, BLOCKS, 128),
            buf(N_FREQ, 3, PER, 128),
            buf(3, N_OWN, 128),
            buf(3, N_OWN, 128),
            buf(N_FREQ, 3, LOCAL, 128),
            dma((8,)),
            dma((2,)),
        ]
        + [dma] * 2
        + [dma((parts,))] * 4
        + [dma((2,))] * 2
        + [dma((parts, 2))] * 2
        + [dma((parts,))] * 6,
        compiler_params=pltpu.CompilerParams(
            collective_id=0, has_side_effects=True, vmem_limit_bytes=56 << 20
        ),
    )(
        omegas, background, block_count, block_owner.reshape(1, BLOCKS), block_local,
        conductivity, source, adjoint,
    )
    return pl.pallas_call(
        settle,
        out_shape=(
            jax.ShapeDtypeStruct(field.shape, F32),
            jax.ShapeDtypeStruct(gradient.shape, F32),
        ),
        in_specs=[hbm] * 2,
        out_specs=(hbm, hbm),
        scratch_shapes=[buf(6, ROWS, LAYER * 128), buf(LOCAL, 384), dma((7,)), dma((7,))],
        compiler_params=pltpu.CompilerParams(vmem_limit_bytes=56 << 20),
    )(field, gradient)


def solution(mesh):
    return jax.shard_map(
        on_device,
        mesh=mesh,
        in_specs=(
            P("snd", None, "mesh", None),
            P("snd", "freq", None, "mesh", None),
            P("freq"),
            P(),
            P(("snd", "mesh"), None),
            P("snd", "mesh", None),
            P("snd", "mesh"),
            P("snd"),
        ),
        out_specs=(P("snd", "freq", None, "mesh", None), P(("snd", "mesh"), None)),
        check_vma=False,
    )
```

```python
import functools
import jax
import jax.numpy as jnp
from jax import lax
from jax.sharding import PartitionSpec as P
from jax.experimental import pallas as pl
from jax.experimental.pallas import tpu as pltpu

NZ = 48
ITERS = 4
ROWS = 8
BLOCKS = 192
LAYER = 24
HALO = ITERS - 1
EXT = ROWS + 2 * HALO
OWN0 = HALO * LAYER
HSZ = HALO * LAYER
ESZ = EXT * LAYER
N_OWN = 128
N_MESH = 4
N_FREQ = 4
PER = BLOCKS // N_FREQ
LOCAL = 64
F32 = jnp.float32
BF16 = jnp.bfloat16
I32 = jnp.int32
MESH = pl.DeviceIdType.MESH
FETCH = ((0, 2), (2, 1))
SUMS = ((0, 2), (2, 1))


def iota(shape, dim):
    return lax.broadcasted_iota(I32, shape, dim)


def onehot(mask):
    return jnp.where(mask, 1.0, 0.0).astype(BF16)


def pick(rows, values):
    high = values.astype(BF16)
    low = (values - high.astype(F32)).astype(BF16)
    dot = functools.partial(jnp.dot, preferred_element_type=F32)
    return dot(rows, high) + dot(rows, low)


def kernel(
    omegas_hbm, background_hbm, count_hbm, owner_hbm, local_hbm, cond_hbm, source_hbm, adjoint_hbm,
    field_hbm, grad_hbm,
    omegas, background, count, owner_in, local_in, cond, grad_out, src_raw, adj_raw, src, adj, sig, wgt, fld, crl,
    ask, wanted, replies, fetched, shared, grads, summed, slots, arrived, partial_,
    in_sem, out_sem, ask_s, ask_r, rep_s, rep_r, sh_s, sh_r, hs_s, hs_r, hw_s, hw_r,
    rs_s, rs_r, gr_s, gr_r, ps_s, ps_r,
):
    s, f, m = lax.axis_index("snd"), lax.axis_index("freq"), lax.axis_index("mesh")
    z, core = s // 2, s % 2
    me = s * N_MESH + m

    def each_peer(act):
        def group(dz, with_self):
            for dm in (2, 1, 3, 0):
                for flip in (0, 1):
                    if with_self and dm == 0 and flip == 0:
                        continue
                    act(((z + dz) % 16) * 2 + (core if flip == 0 else 1 - core), (m + dm) % N_MESH)

        def body(i, carry):
            group(8 + (1 - 2 * (i % 2)) * ((i + 1) // 2), False)
            return carry

        lax.fori_loop(0, 15, body, 0)
        group(0, True)

    barrier = pltpu.get_barrier_semaphore()

    def greet(ps, pm):
        pl.semaphore_signal(barrier, inc=1, device_id={"snd": ps, "mesh": pm}, device_id_type=MESH)

    each_peer(greet)
    for k in range(1, N_FREQ):
        pl.semaphore_signal(
            barrier, inc=1, device_id={"freq": (f + k) % N_FREQ}, device_id_type=MESH
        )

    def remote(a, b, ss, rs, **to):
        return pltpu.make_async_remote_copy(
            src_ref=a, dst_ref=b, send_sem=ss, recv_sem=rs, device_id=to, device_id_type=MESH
        )

    def wait(ref, sem):
        pltpu.make_async_copy(ref, ref, sem).wait()

    load_src = pltpu.make_async_copy(source_hbm.at[0], src_raw, in_sem.at[0])
    load_adj = pltpu.make_async_copy(adjoint_hbm.at[0, 0], adj_raw, in_sem.at[1])
    small = [
        pltpu.make_async_copy(a, b, in_sem.at[2 + i])
        for i, (a, b) in enumerate(
            (
                (owner_hbm, owner_in),
                (local_hbm, local_in),
                (cond_hbm, cond),
                (omegas_hbm, omegas),
                (background_hbm, background),
                (count_hbm, count),
            )
        )
    ]
    for copy in small:
        copy.start()
    load_src.start()
    load_adj.start()
    for copy in small:
        copy.wait()

    eye = iota((BLOCKS, BLOCKS), 0) == iota((BLOCKS, BLOCKS), 1)

    def to_col(row):
        return jnp.sum(jnp.where(eye, row, 0), axis=1, keepdims=True)

    owner_row = owner_in[...]
    owner_col = to_col(owner_row)
    local_col = to_col(local_in[...])
    key_row = owner_row * 256 + iota((1, BLOCKS), 1)
    key_col = owner_col * 256 + iota((BLOCKS, 1), 0)
    pos_row = jnp.sum(jnp.where(key_col < key_row, 1, 0), axis=0, keepdims=True)
    pos_col = jnp.sum(jnp.where(key_row < key_col, 1, 0), axis=1, keepdims=True)
    place_row = (pos_row % N_FREQ) * PER + pos_row // N_FREQ
    place_col = (pos_col % N_FREQ) * PER + pos_col // N_FREQ
    owners = iota((1, N_OWN), 1)
    mine = (owner_col == owners) & (pos_col % N_FREQ == f)
    ask[...] = jnp.sum(jnp.where(mine, local_col + 1, 0), axis=0, keepdims=True)

    def spread(raw, out, first):
        for c in range(6):
            for k in range(LAYER):
                out[c, pl.ds(first + k, ROWS, stride=LAYER), :] = raw[c, :, k * 128 : (k + 1) * 128]

    load_src.wait()
    spread(src_raw, src, OWN0)

    pl.semaphore_wait(barrier, N_OWN - 1 + N_FREQ - 1)

    wanted[pl.ds(me, 1), :] = ask[...]
    each_peer(
        lambda ps, pm: remote(
            ask, wanted.at[pl.ds(me, 1)], ask_s, ask_r, snd=ps, mesh=pm
        ).start()
    )

    up, down = (m + 1) % N_MESH, (m + 3) % N_MESH

    def trade_layers(ref, ss, rs, first, number):
        part = pl.ds(first, number)
        remote(
            ref.at[part, pl.ds(OWN0 + BLOCKS - HSZ, HSZ)], ref.at[part, pl.ds(0, HSZ)],
            ss.at[0], rs.at[0], mesh=up,
        ).start()
        remote(
            ref.at[part, pl.ds(OWN0, HSZ)], ref.at[part, pl.ds(OWN0 + BLOCKS, HSZ)],
            ss.at[1], rs.at[1], mesh=down,
        ).start()

    def layers_in(ref, rs, first, number):
        part = pl.ds(first, number)
        wait(ref.at[part, pl.ds(0, HSZ)], rs.at[0])
        wait(ref.at[part, pl.ds(OWN0 + BLOCKS, HSZ)], rs.at[1])

    def layers_out(ref, ss, first, number):
        part = pl.ds(first, number)
        wait(ref.at[part, pl.ds(OWN0 + BLOCKS - HSZ, HSZ)], ss.at[0])
        wait(ref.at[part, pl.ds(OWN0, HSZ)], ss.at[1])

    trade_layers(src, hs_s, hs_r, 0, 6)

    load_adj.wait()
    spread(adj_raw, adj, 0)

    less_row = jnp.sum(jnp.where(owner_col < owners, 1, 0), axis=0, keepdims=True)
    many_row = jnp.sum(jnp.where(owner_col == owners, 1, 0), axis=0, keepdims=True)
    owners_c = iota((N_OWN, 1), 0)
    less_col = jnp.sum(jnp.where(owner_row < owners_c, 1, 0), axis=1, keepdims=True)
    many_col = jnp.sum(jnp.where(owner_row == owners_c, 1, 0), axis=1, keepdims=True)
    at_col = iota((PER, 1), 0) * N_FREQ + f
    at_row = iota((1, PER), 1) * N_FREQ + f
    squeeze = onehot((at_col >= less_row) & (at_col < less_row + many_row))
    widen = onehot((at_row >= less_col) & (at_row < less_col + many_col))
    unsort = onehot(place_col == iota((1, BLOCKS), 1))
    resort = onehot(iota((BLOCKS, 1), 0) == place_row)

    low_keep = jnp.where(m > 0, 1.0, 0.0)
    high_keep = jnp.where(m < N_MESH - 1, 1.0, 0.0)
    layers_in(src, hs_r, 0, 6)
    for c in range(6):
        src[c, 0:OWN0, :] = src[c, 0:OWN0, :] * low_keep
        src[c, OWN0 + BLOCKS : ESZ, :] = src[c, OWN0 + BLOCKS : ESZ, :] * high_keep

    wait(wanted.at[pl.ds(0, N_OWN - 1)], ask_r)
    asked = jnp.sum(
        jnp.where(iota((N_OWN, N_OWN), 1) == me, wanted[...], 0), axis=1, keepdims=True
    )
    look = onehot(asked - 1 == iota((1, LOCAL), 1))

    def scatter_rows(a, b, ss, rs, first, number):
        part = pl.ds(first, number)
        each_peer(
            lambda ps, pm: remote(
                a.at[part, pl.ds(ps * N_MESH + pm, 1)], b.at[part, pl.ds(me, 1)], ss, rs,
                snd=ps, mesh=pm,
            ).start()
        )
        b[part, pl.ds(me, 1), :] = a[part, pl.ds(me, 1), :]

    for k, (first, number) in enumerate(FETCH):
        for c in range(first, first + number):
            replies[c] = pick(look, cond[:, c * 128 : (c + 1) * 128])
        scatter_rows(replies, fetched, rep_s.at[k], rep_r.at[k], first, number)
    asked_row = jnp.sum(
        jnp.where(iota((N_OWN, N_OWN), 0) == iota((N_OWN, N_OWN), 1), asked, 0), axis=0, keepdims=True
    )

    own_part = pl.ds(pl.multiple_of(f * PER, 8), PER)
    for k, (first, number) in enumerate(FETCH):
        part = pl.ds(first, number)
        wait(fetched.at[part, pl.ds(0, N_OWN - 1)], rep_r.at[k])
        for c in range(first, first + number):
            shared[c, own_part, :] = pick(squeeze, fetched[c])
        for to in range(1, N_FREQ):
            remote(
                shared.at[part, own_part], shared.at[part, own_part], sh_s.at[k], sh_r.at[k],
                freq=(f + to) % N_FREQ,
            ).start()

    live = m * BLOCKS + iota((BLOCKS, 1), 0) < count[0]
    for k, (first, number) in enumerate(FETCH):
        wait(shared.at[pl.ds(first, number), pl.ds(0, BLOCKS - PER)], sh_r.at[k])
        for c in range(first, first + number):
            sig[c, pl.ds(OWN0, BLOCKS), :] = jnp.where(live, pick(unsort, shared[c]), background[c])
        trade_layers(sig, hw_s.at[k], hw_r.at[k], first, number)

    omega = omegas[0]
    shape = (LAYER, 128)
    lane = iota(shape, 1)
    cell = iota(shape, 0) * 128 + lane
    third = cell % NZ
    y_last, z_last = cell >= LAYER * 128 - NZ, third == NZ - 1
    y_first, z_first = cell < NZ, third == 0

    def at(i, offset=0):
        start = i * LAYER
        return pl.ds(pl.multiple_of(start, 8) if offset == 0 else start + offset, LAYER)

    def sy(x, after):
        return jnp.where(y_last, 0.0, pltpu.roll(jnp.where(lane < NZ, after, x), 128 - NZ, 1))

    def sz(x, after):
        return jnp.where(z_last, 0.0, pltpu.roll(jnp.where(lane < 1, after, x), 127, 1))

    def by(x, before):
        return jnp.where(y_first, 0.0, pltpu.roll(jnp.where(lane >= 128 - NZ, before, x), NZ, 1))

    def bz(x, before):
        return jnp.where(z_first, 0.0, pltpu.roll(jnp.where(lane >= 127, before, x), 1, 1))

    def begin(i):
        for c in range(3):
            w = omega * sig[c, at(i), :]
            scale = 0.5 / (16.0 + w * w)
            real, imag = 4.0 * scale, w * scale
            sr, si = src[c, at(i), :], src[c + 3, at(i), :]
            wgt[c, at(i), :] = w
            wgt[c + 3, at(i), :] = real
            wgt[c + 6, at(i), :] = imag
            fld[c, at(i), :] = real * sr + imag * si
            fld[c + 3, at(i), :] = real * si - imag * sr

    def curl(i, keep=None):
        for p in (0, 3):
            ex, ey, ez = (fld[p + c, at(i), :] for c in range(3))
            ax, ay, az = (fld[p + c, at(i, 1), :] for c in range(3))
            ny, nz = fld[p + 1, at(i + 1), :], fld[p + 2, at(i + 1), :]
            hx = (sy(ez, az) - ez) - (sz(ey, ay) - ey)
            hy = (sz(ex, ax) - ex) - (nz - ez)
            hz = (ny - ey) - (sy(ex, ax) - ex)
            for c, h in enumerate((hx, hy, hz)):
                crl[p + c, at(i), :] = h if keep is None else h * keep

    def update(i, keep=None):
        image = []
        for p in (0, 3):
            hx, hy, hz = (crl[p + c, at(i), :] for c in range(3))
            bx, bhy, bhz = (crl[p + c, at(i, -1), :] for c in range(3))
            py, pz = crl[p + 1, at(i - 1), :], crl[p + 2, at(i - 1), :]
            image.append((bz(hy, bhy) - hy) - (by(hz, bhz) - hz))
            image.append((pz - hz) - (bz(hx, bx) - hx))
            image.append((by(hx, bx) - hx) - (py - hy))
        if keep is not None:
            image = [v * keep for v in image]
        for c in range(3):
            w, real, imag = (wgt[c + 3 * k, at(i), :] for k in range(3))
            er, ei = fld[c, at(i), :], fld[c + 3, at(i), :]
            rr = src[c, at(i), :] - image[c] + w * ei
            ri = src[c + 3, at(i), :] - image[c + 3] - w * er
            fld[c, at(i), :] = er + (real * rr + imag * ri)
            fld[c + 3, at(i), :] = ei + (real * ri - imag * rr)

    def loop(lo, hi, act):
        def body(i, carry):
            act(i)
            return carry

        lax.fori_loop(lo, hi, body, 0)

    top = HALO + ROWS
    loop(HALO, top, begin)
    for it in range(1, ITERS):
        loop(HALO + it - 1, top - it, curl)
        loop(HALO + it, top - it, update)

    for k, (first, number) in enumerate(FETCH):
        layers_in(sig, hw_r.at[k], first, number)

    def edge_begin(i):
        begin(i)
        begin(i + top)

    for j in range(HALO):
        edge_begin(j)
    for it in range(1, ITERS):

        def edge_curl(j):
            low = it - 1 + j
            curl(low, jnp.where(low < HALO, low_keep, 1.0))
            curl(top - it + j)

        def edge_update(j):
            high = top - it + j
            update(it + j)
            update(high, jnp.where(high >= top, high_keep, 1.0))

        for j in range(HALO):
            edge_curl(j)
        for j in range(HALO):
            edge_update(j)

    own = pl.ds(OWN0, BLOCKS)
    for k, (first, number) in enumerate(SUMS):
        part = pl.ds(first, number)
        for c in range(first, first + number):
            sens = omega * (adj[c] * fld[c + 3, own, :] - adj[c + 3] * fld[c, own, :])
            grads[c] = pick(resort, jnp.where(live, sens, 0.0))
        for to in range(1, N_FREQ):
            peer = (f + to) % N_FREQ
            remote(
                grads.at[part, pl.ds(pl.multiple_of(peer * PER, 8), PER)], summed.at[f, part],
                rs_s.at[k], rs_r.at[k], freq=peer,
            ).start()
        summed[f, part] = grads[part, own_part, :]

    collect = onehot(asked_row - 1 == iota((LOCAL, 1), 0))
    for k, (first, number) in enumerate(SUMS):
        wait(summed.at[pl.ds(0, N_FREQ - 1), pl.ds(first, number)], rs_r.at[k])
        for c in range(first, first + number):
            total = (summed[0, c] + summed[1, c]) + (summed[2, c] + summed[3, c])
            slots[c] = pick(widen, total)
        scatter_rows(slots, arrived, gr_s.at[k], gr_r.at[k], first, number)

    for c in range(6):
        for k in range(LAYER):
            src_raw[c, :, k * 128 : (k + 1) * 128] = fld[c, pl.ds(OWN0 + k, ROWS, stride=LAYER), :]
    store = pltpu.make_async_copy(src_raw, field_hbm.at[0, 0], out_sem.at[0])
    store.start()

    for k, (first, number) in enumerate(SUMS):
        part = pl.ds(first, number)
        wait(arrived.at[part, pl.ds(0, N_OWN - 1)], gr_r.at[k])
        for c in range(first, first + number):
            partial_[f, c] = pick(collect, arrived[c])
        for to in range(1, N_FREQ):
            remote(
                partial_.at[f, part], partial_.at[f, part], ps_s.at[k], ps_r.at[k],
                freq=(f + to) % N_FREQ,
            ).start()
    for k, (first, number) in enumerate(SUMS):
        wait(partial_.at[pl.ds(0, N_FREQ - 1), pl.ds(first, number)], ps_r.at[k])
        for c in range(first, first + number):
            grad_out[:, c * 128 : (c + 1) * 128] = (partial_[0, c] + partial_[1, c]) + (
                partial_[2, c] + partial_[3, c]
            )
    store_grad = pltpu.make_async_copy(grad_out, grad_hbm, out_sem.at[1])
    store_grad.start()

    wait(wanted.at[pl.ds(0, N_OWN - 1)], ask_s)
    layers_out(src, hs_s, 0, 6)
    for k, (first, number) in enumerate(FETCH):
        part = pl.ds(first, number)
        wait(fetched.at[part, pl.ds(0, N_OWN - 1)], rep_s.at[k])
        wait(shared.at[part, pl.ds(0, BLOCKS - PER)], sh_s.at[k])
        layers_out(sig, hw_s.at[k], first, number)
    for k, (first, number) in enumerate(SUMS):
        part = pl.ds(first, number)
        wait(summed.at[pl.ds(0, N_FREQ - 1), part], rs_s.at[k])
        wait(arrived.at[part, pl.ds(0, N_OWN - 1)], gr_s.at[k])
        wait(partial_.at[pl.ds(0, N_FREQ - 1), part], ps_s.at[k])
    store.wait()
    store_grad.wait()


def settle(field, gradient, field_out, gradient_out, held, held_gradient, sem_in, sem_out):
    ways = [(field.at[0, 0, c], held.at[c], field_out.at[0, 0, c]) for c in range(6)]
    ways.append((gradient, held_gradient, gradient_out))
    loads = [pltpu.make_async_copy(a, b, sem_in.at[i]) for i, (a, b, _) in enumerate(ways)]
    stores = [pltpu.make_async_copy(b, c, sem_out.at[i]) for i, (_, b, c) in enumerate(ways)]
    for load in loads:
        load.start()
    for load, store in zip(loads, stores):
        load.wait()
        store.start()
    for store in stores:
        store.wait()


def on_device(
    source, adjoint, omegas, background, conductivity, block_owner, block_local, block_count
):
    hbm = pl.BlockSpec(memory_space=pltpu.HBM)
    buf = lambda *shape: pltpu.VMEM(shape, F32)
    dma = pltpu.SemaphoreType.DMA
    field, gradient = pl.pallas_call(
        kernel,
        out_shape=(
            jax.ShapeDtypeStruct(adjoint.shape, F32),
            jax.ShapeDtypeStruct(conductivity.shape, F32),
        ),
        in_specs=[hbm] * 8,
        out_specs=(hbm, hbm),
        scratch_shapes=[
            pltpu.SMEM((1,), F32),
            pltpu.SMEM((3,), F32),
            pltpu.SMEM((1,), I32),
            pltpu.VMEM((1, BLOCKS), I32),
            pltpu.VMEM((1, BLOCKS), I32),
            buf(LOCAL, 384),
            buf(LOCAL, 384),
            buf(6, ROWS, LAYER * 128),
            buf(6, ROWS, LAYER * 128),
            buf(6, ESZ, 128),
            buf(6, BLOCKS, 128),
            buf(3, ESZ, 128),
            buf(9, ESZ, 128),
            buf(6, ESZ, 128),
            buf(6, ESZ, 128),
            pltpu.VMEM((1, N_OWN), I32),
            pltpu.VMEM((N_OWN, N_OWN), I32),
            buf(3, N_OWN, 128),
            buf(3, N_OWN, 128),
            buf(3, BLOCKS, 128),
            buf(3, BLOCKS, 128),
            buf(N_FREQ, 3, PER, 128),
            buf(3, N_OWN, 128),
            buf(3, N_OWN, 128),
            buf(N_FREQ, 3, LOCAL, 128),
            dma((8,)),
            dma((2,)),
        ]
        + [dma] * 2
        + [dma((len(FETCH),))] * 4
        + [dma((2,))] * 2
        + [dma((len(FETCH), 2))] * 2
        + [dma((len(SUMS),))] * 6,
        compiler_params=pltpu.CompilerParams(
            collective_id=0, has_side_effects=True, vmem_limit_bytes=56 << 20
        ),
    )(
        omegas, background, block_count, block_owner.reshape(1, BLOCKS), block_local,
        conductivity, source, adjoint,
    )
    return pl.pallas_call(
        settle,
        out_shape=(
            jax.ShapeDtypeStruct(field.shape, F32),
            jax.ShapeDtypeStruct(gradient.shape, F32),
        ),
        in_specs=[hbm] * 2,
        out_specs=(hbm, hbm),
        scratch_shapes=[buf(6, ROWS, LAYER * 128), buf(LOCAL, 384), dma((7,)), dma((7,))],
        compiler_params=pltpu.CompilerParams(vmem_limit_bytes=56 << 20),
    )(field, gradient)


def solution(mesh):
    return jax.shard_map(
        on_device,
        mesh=mesh,
        in_specs=(
            P("snd", None, "mesh", None),
            P("snd", "freq", None, "mesh", None),
            P("freq"),
            P(),
            P(("snd", "mesh"), None),
            P("snd", "mesh", None),
            P("snd", "mesh"),
            P("snd"),
        ),
        out_specs=(P("snd", "freq", None, "mesh", None), P(("snd", "mesh"), None)),
        check_vma=False,
    )
```

```python
import functools
import jax
import jax.numpy as jnp
from jax import lax
from jax.sharding import PartitionSpec as P
from jax.experimental import pallas as pl
from jax.experimental.pallas import tpu as pltpu

NZ = 48
ITERS = 4
ROWS = 8
BLOCKS = 192
LAYER = 24
HALO = ITERS - 1
EXT = ROWS + 2 * HALO
OWN0 = HALO * LAYER
HSZ = HALO * LAYER
ESZ = EXT * LAYER
N_OWN = 128
N_MESH = 4
N_FREQ = 4
PER = BLOCKS // N_FREQ
LOCAL = 64
F32 = jnp.float32
BF16 = jnp.bfloat16
I32 = jnp.int32
MESH = pl.DeviceIdType.MESH
FETCH = ((0, 2), (2, 1))
SUMS = ((0, 1), (1, 1), (2, 1))


def iota(shape, dim):
    return lax.broadcasted_iota(I32, shape, dim)


def onehot(mask):
    return jnp.where(mask, 1.0, 0.0).astype(BF16)


def pick(rows, values):
    high = values.astype(BF16)
    low = (values - high.astype(F32)).astype(BF16)
    dot = functools.partial(jnp.dot, preferred_element_type=F32)
    return dot(rows, high) + dot(rows, low)


def kernel(
    omegas_hbm, background_hbm, count_hbm, owner_hbm, local_hbm, cond_hbm, source_hbm, adjoint_hbm,
    field_hbm, grad_hbm,
    omegas, background, count, owner_in, local_in, cond, grad_out, src_raw, adj_raw, src, adj, sig, wgt, fld, crl,
    ask, wanted, replies, fetched, shared, grads, summed, slots, arrived, partial_,
    in_sem, out_sem, ask_s, ask_r, rep_s, rep_r, sh_s, sh_r, hs_s, hs_r, hw_s, hw_r,
    rs_s, rs_r, gr_s, gr_r, ps_s, ps_r,
):
    s, f, m = lax.axis_index("snd"), lax.axis_index("freq"), lax.axis_index("mesh")
    z, core = s // 2, s % 2
    me = s * N_MESH + m

    def each_peer(act):
        def group(dz, with_self):
            for dm in (2, 1, 3, 0):
                for flip in (0, 1):
                    if with_self and dm == 0 and flip == 0:
                        continue
                    act(((z + dz) % 16) * 2 + (core if flip == 0 else 1 - core), (m + dm) % N_MESH)

        def body(i, carry):
            group(8 + (1 - 2 * (i % 2)) * ((i + 1) // 2), False)
            return carry

        lax.fori_loop(0, 15, body, 0)
        group(0, True)

    barrier = pltpu.get_barrier_semaphore()

    def greet(ps, pm):
        pl.semaphore_signal(barrier, inc=1, device_id={"snd": ps, "mesh": pm}, device_id_type=MESH)

    each_peer(greet)
    for k in range(1, N_FREQ):
        pl.semaphore_signal(
            barrier, inc=1, device_id={"freq": (f + k) % N_FREQ}, device_id_type=MESH
        )

    def remote(a, b, ss, rs, **to):
        return pltpu.make_async_remote_copy(
            src_ref=a, dst_ref=b, send_sem=ss, recv_sem=rs, device_id=to, device_id_type=MESH
        )

    def wait(ref, sem):
        pltpu.make_async_copy(ref, ref, sem).wait()

    load_src = pltpu.make_async_copy(source_hbm.at[0], src_raw, in_sem.at[0])
    load_adj = pltpu.make_async_copy(adjoint_hbm.at[0, 0], adj_raw, in_sem.at[1])
    small = [
        pltpu.make_async_copy(a, b, in_sem.at[2 + i])
        for i, (a, b) in enumerate(
            (
                (owner_hbm, owner_in),
                (local_hbm, local_in),
                (cond_hbm, cond),
                (omegas_hbm, omegas),
                (background_hbm, background),
                (count_hbm, count),
            )
        )
    ]
    for copy in small:
        copy.start()
    load_src.start()
    load_adj.start()
    for copy in small:
        copy.wait()

    eye = iota((BLOCKS, BLOCKS), 0) == iota((BLOCKS, BLOCKS), 1)

    def to_col(row):
        return jnp.sum(jnp.where(eye, row, 0), axis=1, keepdims=True)

    owner_row = owner_in[...]
    owner_col = to_col(owner_row)
    local_col = to_col(local_in[...])
    key_row = owner_row * 256 + iota((1, BLOCKS), 1)
    key_col = owner_col * 256 + iota((BLOCKS, 1), 0)
    pos_row = jnp.sum(jnp.where(key_col < key_row, 1, 0), axis=0, keepdims=True)
    pos_col = jnp.sum(jnp.where(key_row < key_col, 1, 0), axis=1, keepdims=True)
    place_row = (pos_row % N_FREQ) * PER + pos_row // N_FREQ
    place_col = (pos_col % N_FREQ) * PER + pos_col // N_FREQ
    owners = iota((1, N_OWN), 1)
    mine = (owner_col == owners) & (pos_col % N_FREQ == f)
    ask[...] = jnp.sum(jnp.where(mine, local_col + 1, 0), axis=0, keepdims=True)

    def spread(raw, out, first):
        for c in range(6):
            for k in range(LAYER):
                out[c, pl.ds(first + k, ROWS, stride=LAYER), :] = raw[c, :, k * 128 : (k + 1) * 128]

    load_src.wait()
    spread(src_raw, src, OWN0)

    pl.semaphore_wait(barrier, N_OWN - 1 + N_FREQ - 1)

    wanted[pl.ds(me, 1), :] = ask[...]
    each_peer(
        lambda ps, pm: remote(
            ask, wanted.at[pl.ds(me, 1)], ask_s, ask_r, snd=ps, mesh=pm
        ).start()
    )

    up, down = (m + 1) % N_MESH, (m + 3) % N_MESH

    def trade_layers(ref, ss, rs, first, number):
        part = pl.ds(first, number)
        remote(
            ref.at[part, pl.ds(OWN0 + BLOCKS - HSZ, HSZ)], ref.at[part, pl.ds(0, HSZ)],
            ss.at[0], rs.at[0], mesh=up,
        ).start()
        remote(
            ref.at[part, pl.ds(OWN0, HSZ)], ref.at[part, pl.ds(OWN0 + BLOCKS, HSZ)],
            ss.at[1], rs.at[1], mesh=down,
        ).start()

    def layers_in(ref, rs, first, number):
        part = pl.ds(first, number)
        wait(ref.at[part, pl.ds(0, HSZ)], rs.at[0])
        wait(ref.at[part, pl.ds(OWN0 + BLOCKS, HSZ)], rs.at[1])

    def layers_out(ref, ss, first, number):
        part = pl.ds(first, number)
        wait(ref.at[part, pl.ds(OWN0 + BLOCKS - HSZ, HSZ)], ss.at[0])
        wait(ref.at[part, pl.ds(OWN0, HSZ)], ss.at[1])

    trade_layers(src, hs_s, hs_r, 0, 6)

    load_adj.wait()
    spread(adj_raw, adj, 0)

    less_row = jnp.sum(jnp.where(owner_col < owners, 1, 0), axis=0, keepdims=True)
    many_row = jnp.sum(jnp.where(owner_col == owners, 1, 0), axis=0, keepdims=True)
    owners_c = iota((N_OWN, 1), 0)
    less_col = jnp.sum(jnp.where(owner_row < owners_c, 1, 0), axis=1, keepdims=True)
    many_col = jnp.sum(jnp.where(owner_row == owners_c, 1, 0), axis=1, keepdims=True)
    at_col = iota((PER, 1), 0) * N_FREQ + f
    at_row = iota((1, PER), 1) * N_FREQ + f
    squeeze = onehot((at_col >= less_row) & (at_col < less_row + many_row))
    widen = onehot((at_row >= less_col) & (at_row < less_col + many_col))
    unsort = onehot(place_col == iota((1, BLOCKS), 1))
    resort = onehot(iota((BLOCKS, 1), 0) == place_row)

    low_keep = jnp.where(m > 0, 1.0, 0.0)
    high_keep = jnp.where(m < N_MESH - 1, 1.0, 0.0)
    layers_in(src, hs_r, 0, 6)
    for c in range(6):
        src[c, 0:OWN0, :] = src[c, 0:OWN0, :] * low_keep
        src[c, OWN0 + BLOCKS : ESZ, :] = src[c, OWN0 + BLOCKS : ESZ, :] * high_keep

    wait(wanted.at[pl.ds(0, N_OWN - 1)], ask_r)
    asked = jnp.sum(
        jnp.where(iota((N_OWN, N_OWN), 1) == me, wanted[...], 0), axis=1, keepdims=True
    )
    look = onehot(asked - 1 == iota((1, LOCAL), 1))

    def scatter_rows(a, b, ss, rs, first, number):
        part = pl.ds(first, number)
        each_peer(
            lambda ps, pm: remote(
                a.at[part, pl.ds(ps * N_MESH + pm, 1)], b.at[part, pl.ds(me, 1)], ss, rs,
                snd=ps, mesh=pm,
            ).start()
        )
        b[part, pl.ds(me, 1), :] = a[part, pl.ds(me, 1), :]

    for k, (first, number) in enumerate(FETCH):
        for c in range(first, first + number):
            replies[c] = pick(look, cond[:, c * 128 : (c + 1) * 128])
        scatter_rows(replies, fetched, rep_s.at[k], rep_r.at[k], first, number)
    asked_row = jnp.sum(
        jnp.where(iota((N_OWN, N_OWN), 0) == iota((N_OWN, N_OWN), 1), asked, 0), axis=0, keepdims=True
    )

    own_part = pl.ds(pl.multiple_of(f * PER, 8), PER)
    for k, (first, number) in enumerate(FETCH):
        part = pl.ds(first, number)
        wait(fetched.at[part, pl.ds(0, N_OWN - 1)], rep_r.at[k])
        for c in range(first, first + number):
            shared[c, own_part, :] = pick(squeeze, fetched[c])
        for to in range(1, N_FREQ):
            remote(
                shared.at[part, own_part], shared.at[part, own_part], sh_s.at[k], sh_r.at[k],
                freq=(f + to) % N_FREQ,
            ).start()

    live = m * BLOCKS + iota((BLOCKS, 1), 0) < count[0]
    for k, (first, number) in enumerate(FETCH):
        wait(shared.at[pl.ds(first, number), pl.ds(0, BLOCKS - PER)], sh_r.at[k])
        for c in range(first, first + number):
            sig[c, pl.ds(OWN0, BLOCKS), :] = jnp.where(live, pick(unsort, shared[c]), background[c])
        trade_layers(sig, hw_s.at[k], hw_r.at[k], first, number)

    omega = omegas[0]
    shape = (LAYER, 128)
    lane = iota(shape, 1)
    cell = iota(shape, 0) * 128 + lane
    third = cell % NZ
    y_last, z_last = cell >= LAYER * 128 - NZ, third == NZ - 1
    y_first, z_first = cell < NZ, third == 0

    def at(i, offset=0):
        start = i * LAYER
        return pl.ds(pl.multiple_of(start, 8) if offset == 0 else start + offset, LAYER)

    def sy(x, after):
        return jnp.where(y_last, 0.0, pltpu.roll(jnp.where(lane < NZ, after, x), 128 - NZ, 1))

    def sz(x, after):
        return jnp.where(z_last, 0.0, pltpu.roll(jnp.where(lane < 1, after, x), 127, 1))

    def by(x, before):
        return jnp.where(y_first, 0.0, pltpu.roll(jnp.where(lane >= 128 - NZ, before, x), NZ, 1))

    def bz(x, before):
        return jnp.where(z_first, 0.0, pltpu.roll(jnp.where(lane >= 127, before, x), 1, 1))

    def begin(i):
        for c in range(3):
            w = omega * sig[c, at(i), :]
            scale = 0.5 / (16.0 + w * w)
            real, imag = 4.0 * scale, w * scale
            sr, si = src[c, at(i), :], src[c + 3, at(i), :]
            wgt[c, at(i), :] = w
            wgt[c + 3, at(i), :] = real
            wgt[c + 6, at(i), :] = imag
            fld[c, at(i), :] = real * sr + imag * si
            fld[c + 3, at(i), :] = real * si - imag * sr

    def curl(i, keep=None):
        for p in (0, 3):
            ex, ey, ez = (fld[p + c, at(i), :] for c in range(3))
            ax, ay, az = (fld[p + c, at(i, 1), :] for c in range(3))
            ny, nz = fld[p + 1, at(i + 1), :], fld[p + 2, at(i + 1), :]
            hx = (sy(ez, az) - ez) - (sz(ey, ay) - ey)
            hy = (sz(ex, ax) - ex) - (nz - ez)
            hz = (ny - ey) - (sy(ex, ax) - ex)
            for c, h in enumerate((hx, hy, hz)):
                crl[p + c, at(i), :] = h if keep is None else h * keep

    def update(i, keep=None):
        image = []
        for p in (0, 3):
            hx, hy, hz = (crl[p + c, at(i), :] for c in range(3))
            bx, bhy, bhz = (crl[p + c, at(i, -1), :] for c in range(3))
            py, pz = crl[p + 1, at(i - 1), :], crl[p + 2, at(i - 1), :]
            image.append((bz(hy, bhy) - hy) - (by(hz, bhz) - hz))
            image.append((pz - hz) - (bz(hx, bx) - hx))
            image.append((by(hx, bx) - hx) - (py - hy))
        if keep is not None:
            image = [v * keep for v in image]
        for c in range(3):
            w, real, imag = (wgt[c + 3 * k, at(i), :] for k in range(3))
            er, ei = fld[c, at(i), :], fld[c + 3, at(i), :]
            rr = src[c, at(i), :] - image[c] + w * ei
            ri = src[c + 3, at(i), :] - image[c + 3] - w * er
            fld[c, at(i), :] = er + (real * rr + imag * ri)
            fld[c + 3, at(i), :] = ei + (real * ri - imag * rr)

    def loop(lo, hi, act):
        def body(i, carry):
            act(i)
            return carry

        lax.fori_loop(lo, hi, body, 0)

    top = HALO + ROWS
    loop(HALO, top, begin)
    for it in range(1, ITERS):
        loop(HALO + it - 1, top - it, curl)
        loop(HALO + it, top - it, update)

    for k, (first, number) in enumerate(FETCH):
        layers_in(sig, hw_r.at[k], first, number)

    def edge_begin(i):
        begin(i)
        begin(i + top)

    for j in range(HALO):
        edge_begin(j)
    for it in range(1, ITERS):

        def edge_curl(j):
            low = it - 1 + j
            curl(low, jnp.where(low < HALO, low_keep, 1.0))
            curl(top - it + j)

        def edge_update(j):
            high = top - it + j
            update(it + j)
            update(high, jnp.where(high >= top, high_keep, 1.0))

        for j in range(HALO):
            edge_curl(j)
        for j in range(HALO):
            edge_update(j)

    own = pl.ds(OWN0, BLOCKS)
    for k, (first, number) in enumerate(SUMS):
        part = pl.ds(first, number)
        for c in range(first, first + number):
            sens = omega * (adj[c] * fld[c + 3, own, :] - adj[c + 3] * fld[c, own, :])
            grads[c] = pick(resort, jnp.where(live, sens, 0.0))
        for to in range(1, N_FREQ):
            peer = (f + to) % N_FREQ
            remote(
                grads.at[part, pl.ds(pl.multiple_of(peer * PER, 8), PER)], summed.at[f, part],
                rs_s.at[k], rs_r.at[k], freq=peer,
            ).start()
        summed[f, part] = grads[part, own_part, :]

    collect = onehot(asked_row - 1 == iota((LOCAL, 1), 0))
    for k, (first, number) in enumerate(SUMS):
        wait(summed.at[pl.ds(0, N_FREQ - 1), pl.ds(first, number)], rs_r.at[k])
        for c in range(first, first + number):
            total = (summed[0, c] + summed[1, c]) + (summed[2, c] + summed[3, c])
            slots[c] = pick(widen, total)
        scatter_rows(slots, arrived, gr_s.at[k], gr_r.at[k], first, number)

    for c in range(6):
        for k in range(LAYER):
            src_raw[c, :, k * 128 : (k + 1) * 128] = fld[c, pl.ds(OWN0 + k, ROWS, stride=LAYER), :]
    store = pltpu.make_async_copy(src_raw, field_hbm.at[0, 0], out_sem.at[0])
    store.start()

    for k, (first, number) in enumerate(SUMS):
        part = pl.ds(first, number)
        wait(arrived.at[part, pl.ds(0, N_OWN - 1)], gr_r.at[k])
        for c in range(first, first + number):
            partial_[f, c] = pick(collect, arrived[c])
        for to in range(1, N_FREQ):
            remote(
                partial_.at[f, part], partial_.at[f, part], ps_s.at[k], ps_r.at[k],
                freq=(f + to) % N_FREQ,
            ).start()
    for k, (first, number) in enumerate(SUMS):
        wait(partial_.at[pl.ds(0, N_FREQ - 1), pl.ds(first, number)], ps_r.at[k])
        for c in range(first, first + number):
            grad_out[:, c * 128 : (c + 1) * 128] = (partial_[0, c] + partial_[1, c]) + (
                partial_[2, c] + partial_[3, c]
            )
    store_grad = pltpu.make_async_copy(grad_out, grad_hbm, out_sem.at[1])
    store_grad.start()

    wait(wanted.at[pl.ds(0, N_OWN - 1)], ask_s)
    layers_out(src, hs_s, 0, 6)
    for k, (first, number) in enumerate(FETCH):
        part = pl.ds(first, number)
        wait(fetched.at[part, pl.ds(0, N_OWN - 1)], rep_s.at[k])
        wait(shared.at[part, pl.ds(0, BLOCKS - PER)], sh_s.at[k])
        layers_out(sig, hw_s.at[k], first, number)
    for k, (first, number) in enumerate(SUMS):
        part = pl.ds(first, number)
        wait(summed.at[pl.ds(0, N_FREQ - 1), part], rs_s.at[k])
        wait(arrived.at[part, pl.ds(0, N_OWN - 1)], gr_s.at[k])
        wait(partial_.at[pl.ds(0, N_FREQ - 1), part], ps_s.at[k])
    store.wait()
    store_grad.wait()


def settle(field, gradient, field_out, gradient_out, held, held_gradient, sem_in, sem_out):
    ways = [(field.at[0, 0, c], held.at[c], field_out.at[0, 0, c]) for c in range(6)]
    ways.append((gradient, held_gradient, gradient_out))
    loads = [pltpu.make_async_copy(a, b, sem_in.at[i]) for i, (a, b, _) in enumerate(ways)]
    stores = [pltpu.make_async_copy(b, c, sem_out.at[i]) for i, (_, b, c) in enumerate(ways)]
    for load in loads:
        load.start()
    for load, store in zip(loads, stores):
        load.wait()
        store.start()
    for store in stores:
        store.wait()


def on_device(
    source, adjoint, omegas, background, conductivity, block_owner, block_local, block_count
):
    hbm = pl.BlockSpec(memory_space=pltpu.HBM)
    buf = lambda *shape: pltpu.VMEM(shape, F32)
    dma = pltpu.SemaphoreType.DMA
    field, gradient = pl.pallas_call(
        kernel,
        out_shape=(
            jax.ShapeDtypeStruct(adjoint.shape, F32),
            jax.ShapeDtypeStruct(conductivity.shape, F32),
        ),
        in_specs=[hbm] * 8,
        out_specs=(hbm, hbm),
        scratch_shapes=[
            pltpu.SMEM((1,), F32),
            pltpu.SMEM((3,), F32),
            pltpu.SMEM((1,), I32),
            pltpu.VMEM((1, BLOCKS), I32),
            pltpu.VMEM((1, BLOCKS), I32),
            buf(LOCAL, 384),
            buf(LOCAL, 384),
            buf(6, ROWS, LAYER * 128),
            buf(6, ROWS, LAYER * 128),
            buf(6, ESZ, 128),
            buf(6, BLOCKS, 128),
            buf(3, ESZ, 128),
            buf(9, ESZ, 128),
            buf(6, ESZ, 128),
            buf(6, ESZ, 128),
            pltpu.VMEM((1, N_OWN), I32),
            pltpu.VMEM((N_OWN, N_OWN), I32),
            buf(3, N_OWN, 128),
            buf(3, N_OWN, 128),
            buf(3, BLOCKS, 128),
            buf(3, BLOCKS, 128),
            buf(N_FREQ, 3, PER, 128),
            buf(3, N_OWN, 128),
            buf(3, N_OWN, 128),
            buf(N_FREQ, 3, LOCAL, 128),
            dma((8,)),
            dma((2,)),
        ]
        + [dma] * 2
        + [dma((len(FETCH),))] * 4
        + [dma((2,))] * 2
        + [dma((len(FETCH), 2))] * 2
        + [dma((len(SUMS),))] * 6,
        compiler_params=pltpu.CompilerParams(
            collective_id=0, has_side_effects=True, vmem_limit_bytes=56 << 20
        ),
    )(
        omegas, background, block_count, block_owner.reshape(1, BLOCKS), block_local,
        conductivity, source, adjoint,
    )
    return pl.pallas_call(
        settle,
        out_shape=(
            jax.ShapeDtypeStruct(field.shape, F32),
            jax.ShapeDtypeStruct(gradient.shape, F32),
        ),
        in_specs=[hbm] * 2,
        out_specs=(hbm, hbm),
        scratch_shapes=[buf(6, ROWS, LAYER * 128), buf(LOCAL, 384), dma((7,)), dma((7,))],
        compiler_params=pltpu.CompilerParams(vmem_limit_bytes=56 << 20),
    )(field, gradient)


def solution(mesh):
    return jax.shard_map(
        on_device,
        mesh=mesh,
        in_specs=(
            P("snd", None, "mesh", None),
            P("snd", "freq", None, "mesh", None),
            P("freq"),
            P(),
            P(("snd", "mesh"), None),
            P("snd", "mesh", None),
            P("snd", "mesh"),
            P("snd"),
        ),
        out_specs=(P("snd", "freq", None, "mesh", None), P(("snd", "mesh"), None)),
        check_vma=False,
    )
```
